512 devices in a mesh: dp: 32 (over y, x), head: 16 (over z, core).
Axes of the slice: x: 4, y: 8, z: 8, core: 2. Of those that a mesh axis runs over, the one named last changes fastest.
Arguments:
- queries: bfloat16 [64, 1024, 8192], P('dp', 'head'), may hold values from -6 to 6
- keys: bfloat16 [64, 1024, 1024], P('dp', 'head'), may hold values from -6 to 6
- values: bfloat16 [64, 1024, 1024], P('dp', 'head'), may hold values from -6 to 6
- segments: int32 [64, 1024], P('dp', 'head'), may hold values from 0 to 3, never falling along the last dimension, each value on 1 to 512 neighbouring positions
- modality: int32 [64, 1024], P('dp', 'head'), may hold values from 0 to 1, as said below
- q_scale: float32 [2, 64, 128], P(None, None, 'dp'), may hold values from 0.5 to 5
- q_shift: float32 [2, 64, 128], P(None, None, 'dp'), may hold values from -1.5 to 1.5
- k_scale: float32 [2, 8, 128], P(None, None, 'dp'), may hold values from 0.5 to 5
- k_shift: float32 [2, 8, 128], P(None, None, 'dp'), may hold values from -1.5 to 1.5
Outputs:
- attended: bfloat16 [64, 1024, 8192], P('dp', 'head')
The draws below stay inside these ranges and needn't reach their ends.
Inputs may be any that keep to these rules, and one draw needn't show every extreme that they name: `modality`: constant over each aligned run of 128 positions of a pack.
All inputs are finite; a program needn't handle non-finite values.
Results may differ from the reference program's by a relative error of at most 0.012.
Values may be sent and summed in bfloat16 or wider, within the bound.
No kernel may reach another device: no remote copies, remote signals or barrier semaphores. Data moves between devices by JAX's collectives and lax.ppermute only.
A program may use at most 128 MiB of HBM per device.

```python
import math
import jax
import jax.numpy as jnp
import numpy as np
from jax import lax

HEADS = 64
KV = 8
HD = 128
LEN = 1024
BLOCK = 128
DOCS = 4
DOC_MOST = 512
PACKS = 64


def shared_keys(key):
    base = jnp.clip(jax.random.normal(key, (PACKS, LEN, KV * HD), jnp.float32), -6.0, 6.0)
    return base


def draw_keys(key, part):
    base = shared_keys(key)
    return base.astype(jnp.bfloat16)


def draw_queries(key, part):
    key = jax.random.fold_in(key, 5)
    fresh = jnp.clip(jax.random.normal(key, (PACKS, LEN, HEADS * HD), jnp.float32), -6.0, 6.0)
    return fresh.astype(jnp.bfloat16)


def draw_modality(key, part):
    key = jax.random.fold_in(key, 7)
    blocks = jax.random.randint(key, (PACKS, LEN // BLOCK), 0, 2)
    blocks = blocks.at[0, 0].set(0).at[0, 1].set(1)
    return jnp.repeat(blocks, BLOCK, axis=1).astype(jnp.int32)


def draw_q_scale(key, part):
    key = jax.random.fold_in(key, 11)
    return jnp.exp(jax.random.uniform(key, (2, HEADS, HD), jnp.float32, math.log(0.5), math.log(2.0)))


def draw_k_scale(key, part):
    key = jax.random.fold_in(key, 13)
    return jnp.exp(jax.random.uniform(key, (2, KV, HD), jnp.float32, math.log(0.5), math.log(2.0)))


def block_levels(own_key, shape, split, low, largest):
    factor_of = 1.0
    for axis_at, shards_of in split:
        steps = jax.random.uniform(jax.random.fold_in(jax.random.fold_in(own_key, 6), axis_at), (shards_of,), jnp.float32, low / len(split), largest / len(split))
        factor_of = factor_of * jnp.repeat(jnp.exp(steps), shape[axis_at] // shards_of).reshape((-1,) + (1,) * (len(shape) - 1 - axis_at))
    return factor_of


def profile(number_of, total, reach, lean):
    weights = [(1 << 20) // math.isqrt(standing ** lean) + 1 for standing in range(2, number_of + 1)]
    rest, given = total - reach - (number_of - 1), [1] * (number_of - 1)
    while rest > 0:
        movable = [i for i in range(number_of - 1) if given[i] < reach]
        mass, budget = sum([weights[i] for i in movable]), rest
        for i in movable:
            extra = min(reach - given[i], max(1, budget * weights[i] // mass), rest)
            given[i] = given[i] + extra
            rest = rest - extra
    return np.array([reach] + given)


def uneven(own_key, number_of, total, reach, lean):
    if number_of == 2:
        one = jax.random.randint(own_key, (), max(1, total - reach), min(reach, total - 1) + 1)
        return jnp.stack([one, total - one])
    sizes = jnp.asarray(profile(number_of, total, reach, lean), jnp.int32)
    twos = (number_of - 1) // 2
    source_of, taker = sizes[1:1 + 2 * twos:2], sizes[2:2 + 2 * twos:2]
    slack = jnp.minimum(source_of - 1, reach - taker)
    shifted = jax.random.randint(jax.random.fold_in(own_key, 1), (twos,), 0, 1 << 20) % (slack + 1)
    sizes = sizes.at[1:1 + 2 * twos:2].set(source_of - shifted).at[2:2 + 2 * twos:2].set(taker + shifted)
    return sizes[jax.random.permutation(jax.random.fold_in(own_key, 2), number_of)]


def bell_draw(key, extent, width, limit, shards=(), kind=jnp.bfloat16):
    values = width * jax.random.normal(key, extent, jnp.float32)
    if shards:
        values = values * block_levels(key, extent, shards, -0.22, 0.18)
    return jnp.clip(values, -limit, limit).astype(kind)


def setup_inputs(seed: int = 0) -> dict:
    streams_of = jax.random.split(jax.random.key(seed), 10)
    return {
        "queries": draw_queries(jax.random.fold_in(streams_of[9], 71), 0),
        "keys": draw_keys(jax.random.fold_in(streams_of[9], 71), 0),
        "values": bell_draw(streams_of[2], (PACKS, LEN, KV * HD), 1.0, 6.0, ((0, 32), (1, 16))),
        "segments": jax.vmap(lambda own: jnp.searchsorted(jnp.cumsum(uneven(own, DOCS, LEN, DOC_MOST, 2)), jnp.arange(LEN), side="right"))(jax.random.split(streams_of[3], PACKS)).reshape((PACKS, LEN)).astype(jnp.int32),
        "modality": draw_modality(jax.random.fold_in(streams_of[9], 71), 0),
        "q_scale": draw_q_scale(jax.random.fold_in(streams_of[9], 71), 0),
        "q_shift": bell_draw(streams_of[6], (2, HEADS, HD), 0.3, 1.5, ((2, 32),), jnp.float32),
        "k_scale": draw_k_scale(jax.random.fold_in(streams_of[9], 71), 0),
        "k_shift": bell_draw(streams_of[8], (2, KV, HD), 0.3, 1.5, ((2, 32),), jnp.float32),
    }


def normalize(field, labels, scale, shift):
    mean = lax.optimization_barrier(jnp.mean(field, axis=-1, keepdims=True))
    center = field - mean
    spread = lax.optimization_barrier(jnp.mean(center * center, axis=-1, keepdims=True))
    picked = (labels == 1)[:, None, None]
    gains = jnp.where(picked, scale[1], scale[0])
    offsets = jnp.where(picked, shift[1], shift[0])
    return (center * lax.rsqrt(spread + 1e-05) * gains + offsets).astype(jnp.bfloat16)

def reference(queries, keys, values, segments, modality, q_scale, q_shift, k_scale, k_shift):
    group = HEADS // KV
    positions = jnp.arange(LEN)
    causal = positions[None, :] <= positions[:, None]

    def one_pack(item):
        query, key_rows, value_rows, seg, labels = item
        qn = normalize(query.astype(jnp.float32).reshape(LEN, HEADS, HD), labels, q_scale, q_shift)
        kn = normalize(key_rows.astype(jnp.float32).reshape(LEN, KV, HD), labels, k_scale, k_shift)
        qg = qn.astype(jnp.float32).reshape(LEN, KV, group, HD)
        scores = jnp.einsum('skgd,tkd->kgst', qg, kn.astype(jnp.float32)) * HD ** (-0.5)
        allowed = causal & (seg[:, None] == seg[None, :])
        scores = jnp.where(allowed, scores, -jnp.inf)
        top = lax.optimization_barrier(jnp.max(scores, axis=-1, keepdims=True))
        weights = jnp.exp(scores - top)
        weights = (weights / lax.optimization_barrier(jnp.sum(weights, axis=-1, keepdims=True))).astype(jnp.bfloat16)
        vh = value_rows.astype(jnp.float32).reshape(LEN, KV, HD)
        mixed = jnp.einsum('kgst,tkd->skgd', weights.astype(jnp.float32), vh)
        return mixed.reshape(LEN, HEADS * HD).astype(jnp.bfloat16)
    return lax.map(one_pack, (queries, keys, values, segments, modality))
```

```python
import functools
import math

import jax
import jax.numpy as jnp
from jax import lax
from jax.experimental import pallas as pl
from jax.experimental.pallas import tpu as pltpu
from jax.sharding import PartitionSpec as P

KV = 8
GROUP = 8
HD = 128
ROWS = 64
META = 16
ROWS_ALL = 2 * ROWS + META
PARAMS = 384
STRAIGHT = 5
MASKED = -1e30


def pairs(hops, count):
    return [(2 * z + c, 2 * (z + hops) + c) for z in range(count // 2 - hops) for c in (0, 1)]


def normed(x, gain, shift):
    center = x - jnp.mean(x, axis=-1, keepdims=True)
    spread = jnp.mean(center * center, axis=-1, keepdims=True)
    return (center * lax.rsqrt(spread + 1e-05) * gain + shift).astype(jnp.bfloat16)


def attend_kernel(count, q_ref, *refs):
    chunks = [(ref, 0) for ref in refs[: STRAIGHT]]
    chunks += [(refs[STRAIGHT], i * ROWS_ALL) for i in range(count - STRAIGHT)]
    params_ref = refs[STRAIGHT + 1]
    out_ref = refs[-1]
    table = params_ref[...].T

    def pick(image, first, second):
        return jnp.where(image, table[second], table[first])

    metas = [c[at + 2 * ROWS : at + ROWS_ALL, :HD].astype(jnp.float32) for c, at in chunks]
    images = [meta[1:2] > 0.5 for meta in metas]

    span = ROWS * count
    key_seg = jnp.concatenate([meta[0:1, :ROWS] for meta in metas], axis=1)
    key_block = jnp.concatenate([meta[2:3, :ROWS] for meta in metas], axis=1)
    query_seg = jnp.broadcast_to(metas[0][0:1], (HD, HD)).T[:ROWS, 0:1]
    query_block = metas[0][2:3, 0:1]
    key_at = lax.broadcasted_iota(jnp.int32, (ROWS, span), 1)
    query_at = lax.broadcasted_iota(jnp.int32, (ROWS, span), 0)
    past = ((key_at >= ROWS) & (key_block < query_block)) | (key_at <= query_at)
    bias = jnp.where((query_seg == key_seg) & past, 0.0, MASKED)

    for j in range(KV):
        lanes = slice(j * HD, (j + 1) * HD)
        k_normed = []
        for (c, at), image in zip(chunks, images):
            gain = pick(image, slice(256 + j, 257 + j), slice(264 + j, 265 + j))
            shift = pick(image, slice(272 + j, 273 + j), slice(280 + j, 281 + j))
            k_normed.append(normed(c[at : at + ROWS, lanes].astype(jnp.float32), gain, shift))
        keys = jnp.concatenate(k_normed, axis=0)
        values = jnp.concatenate(
            [c[at + ROWS : at + 2 * ROWS, lanes] for c, at in chunks], axis=0
        )
        values = jnp.concatenate([values, jnp.ones_like(values)], axis=1)

        first = GROUP * j
        gains = pick(images[0], slice(first, first + 8), slice(64 + first, 72 + first))
        shifts = pick(images[0], slice(128 + first, 136 + first), slice(192 + first, 200 + first))
        queries = jnp.concatenate(
            [
                normed(
                    q_ref[0, :, (first + h) * HD : (first + h + 1) * HD].astype(jnp.float32),
                    gains[h : h + 1],
                    shifts[h : h + 1],
                )
                for h in range(GROUP)
            ],
            axis=0,
        )
        scores = lax.dot_general(
            queries, keys, (((1,), (1,)), ((), ())), preferred_element_type=jnp.float32
        ) * (HD**-0.5 * math.log2(math.e))
        scores = (scores.reshape(GROUP, ROWS, span) + bias[None]).reshape(GROUP * ROWS, span)
        weights = jnp.exp2(scores - jnp.max(scores, axis=-1, keepdims=True))
        mixed = jnp.dot(weights.astype(jnp.bfloat16), values, preferred_element_type=jnp.float32)
        result = (mixed[:, :HD] * (1.0 / mixed[:, HD:])).astype(out_ref.dtype)
        for h in range(GROUP):
            lane = (first + h) * HD
            out_ref[0, :, lane : lane + HD] = result[h * ROWS : (h + 1) * ROWS]


def attend(pack, queries, straight, crossed, params, earlier):
    count = len(straight) + crossed.shape[0] // ROWS_ALL
    wide = queries.shape[2]
    span = count * ROWS
    in_specs = [pl.BlockSpec((1, ROWS, wide), lambda i: (pack, 0, 0))]
    in_specs += [pl.BlockSpec(x.shape, lambda i: (0, 0)) for x in (*straight, crossed)]
    in_specs += [pl.BlockSpec((HD, PARAMS), lambda i: (0, 0))]
    operands = [queries, *straight, crossed, params]
    aliases = {}
    if earlier is not None:
        aliases = {len(operands): 0}
        operands.append(earlier)
        in_specs.append(pl.BlockSpec(memory_space=pl.ANY))
    return pl.pallas_call(
        functools.partial(attend_kernel, count),
        grid=(1,),
        in_specs=in_specs,
        out_specs=pl.BlockSpec((1, ROWS, wide), lambda i: (pack, 0, 0)),
        out_shape=jax.ShapeDtypeStruct(queries.shape, queries.dtype),
        input_output_aliases=aliases,
        compiler_params=pltpu.CompilerParams(vmem_limit_bytes=40 * 1024 * 1024),
        cost_estimate=pl.CostEstimate(
            flops=KV * GROUP * ROWS * span * HD * 6,
            bytes_accessed=2 * ROWS * wide * 2 + count * ROWS_ALL * KV * HD * 2,
            transcendentals=KV * GROUP * ROWS * span,
        ),
        name="attend",
    )(*operands)


def gather_params(q_scale, q_shift, k_scale, k_shift):
    copies = lax.axis_size("dp")
    width = q_scale.shape[2]
    mine = jnp.concatenate(
        [x.reshape(-1, width) for x in (q_scale, q_shift, k_scale, k_shift)], axis=0
    ).T
    mine = jnp.pad(mine, ((0, 0), (0, PARAMS - mine.shape[1])))
    sent = jnp.broadcast_to(mine[None], (copies, *mine.shape))
    whole = lax.all_to_all(sent, "dp", split_axis=0, concat_axis=0, tiled=True)
    return whole.reshape(copies * width, PARAMS)


def on_device(queries, keys, values, segments, modality, q_scale, q_shift, k_scale, k_shift):
    count = lax.axis_size("head")
    packs = queries.shape[0]
    place = lax.axis_index("head")
    odd = place % 2 == 1
    swap = [(i, i ^ 1) for i in range(count)]

    def send(x, hops):
        return lax.ppermute(x, "head", pairs(hops, count))

    def cross(x):
        return lax.ppermute(x, "head", swap)

    marks = jnp.concatenate([segments + 1, jnp.zeros_like(segments)], axis=1)
    marks = jnp.tile(marks, (1, KV))
    kinds = jnp.broadcast_to(modality[:, :1], marks.shape)
    places = jnp.broadcast_to(place.astype(marks.dtype), marks.shape)
    meta = jnp.stack([marks, kinds, places], axis=1).astype(keys.dtype)
    meta = jnp.pad(meta, ((0, 0), (0, META - 3), (0, 0)))
    own = [jnp.concatenate([keys[p], values[p], meta[p]], axis=0) for p in range(packs)]

    params = gather_params(q_scale, q_shift, k_scale, k_shift)
    first = [send(x, 1) for x in own]
    second = [send(x, 1) for x in first]
    second[-1], params = lax.optimization_barrier((second[-1], params))
    third = [send(x, 1) for x in second]
    fourth = [send(x, 1) for x in third]
    out = None
    crossed = []
    for p in range(packs):
        lacking = jnp.where(odd, fourth[p], own[p])
        crossed.append(cross(jnp.concatenate([first[p], second[p], third[p], lacking], axis=0)))
    for p in range(packs):
        straight = [own[p], first[p], second[p], third[p], fourth[p]]
        out = attend(p, queries, straight, crossed[p], params, out)
    return out


def solution(mesh):
    rows = P("dp", "head", None)
    marks = P("dp", "head")
    norms = P(None, None, "dp")
    placed = (rows, rows, rows, marks, marks, norms, norms, norms, norms)
    return jax.shard_map(
        on_device, mesh=mesh, in_specs=placed, out_specs=rows, check_vma=False
    )
```

```python
import functools
import math

import jax
import jax.numpy as jnp
from jax import lax
from jax.experimental import pallas as pl
from jax.experimental.pallas import tpu as pltpu
from jax.sharding import PartitionSpec as P

KV = 8
GROUP = 8
HD = 128
ROWS = 64
META = 16
MARKS = 3
MARKED_ROWS = 2 * ROWS + META
PARAMS = 384
WINDOW = 9
MASKED = -1e30


def pairs(chips, hops, count):
    ring = count // 2
    return [(2 * (z % ring) + c, 2 * ((z + hops) % ring) + c) for z in chips for c in (0, 1)]


def normed(x, gain, shift):
    center = x - jnp.mean(x, axis=-1, keepdims=True)
    spread = jnp.mean(center * center, axis=-1, keepdims=True)
    return (center * lax.rsqrt(spread + 1e-05) * gain + shift).astype(jnp.bfloat16)


def attend_kernel(pack, blocks, q_ref, *refs):
    meta_refs = refs[:WINDOW]
    chunks = [(refs[WINDOW + i], at) for i, at in blocks]
    params_ref = refs[WINDOW + 1 + blocks[-1][0]]
    out_ref = refs[-1]
    table = params_ref[...].T

    def pick(image, first, second):
        return jnp.where(image, table[second], table[first])

    marks = slice(MARKS * pack, MARKS * (pack + 1))
    metas = [ref[...].astype(jnp.float32)[marks] for ref in meta_refs]
    images = [meta[1:2] > 0.5 for meta in metas]

    span = ROWS * WINDOW
    key_seg = jnp.concatenate([meta[0:1, :ROWS] for meta in metas], axis=1)
    key_block = jnp.concatenate([meta[2:3, :ROWS] for meta in metas], axis=1)
    query_seg = jnp.broadcast_to(metas[0][0:1], (HD, HD)).T[:ROWS, 0:1]
    query_block = metas[0][2:3, 0:1]
    key_at = lax.broadcasted_iota(jnp.int32, (ROWS, span), 1)
    query_at = lax.broadcasted_iota(jnp.int32, (ROWS, span), 0)
    past = ((key_at >= ROWS) & (key_block < query_block)) | (key_at <= query_at)
    bias = jnp.where((query_seg == key_seg) & past, 0.0, MASKED)

    for j in range(KV):
        lanes = slice(j * HD, (j + 1) * HD)
        k_normed = []
        for (ref, at), image in zip(chunks, images):
            gain = pick(image, slice(256 + j, 257 + j), slice(264 + j, 265 + j))
            shift = pick(image, slice(272 + j, 273 + j), slice(280 + j, 281 + j))
            k_normed.append(normed(ref[at : at + ROWS, lanes].astype(jnp.float32), gain, shift))
        keys = jnp.concatenate(k_normed, axis=0)
        values = jnp.concatenate(
            [ref[at + ROWS : at + 2 * ROWS, lanes] for ref, at in chunks], axis=0
        )
        values = jnp.concatenate([values, jnp.ones_like(values)], axis=1)

        first = GROUP * j
        gains = pick(images[0], slice(first, first + 8), slice(64 + first, 72 + first))
        shifts = pick(images[0], slice(128 + first, 136 + first), slice(192 + first, 200 + first))
        queries = jnp.concatenate(
            [
                normed(
                    q_ref[:, (first + h) * HD : (first + h + 1) * HD].astype(jnp.float32),
                    gains[h : h + 1],
                    shifts[h : h + 1],
                )
                for h in range(GROUP)
            ],
            axis=0,
        )
        scores = lax.dot_general(
            queries, keys, (((1,), (1,)), ((), ())), preferred_element_type=jnp.float32
        ) * (HD**-0.5 * math.log2(math.e))
        scores = (scores.reshape(GROUP, ROWS, span) + bias[None]).reshape(GROUP * ROWS, span)
        weights = jnp.exp2(scores - jnp.max(scores, axis=-1, keepdims=True))
        mixed = jnp.dot(weights.astype(jnp.bfloat16), values, preferred_element_type=jnp.float32)
        result = (mixed[:, :HD] * (1.0 / mixed[:, HD:])).astype(out_ref.dtype)
        for h in range(GROUP):
            lane = (first + h) * HD
            out_ref[:, lane : lane + HD] = result[h * ROWS : (h + 1) * ROWS]


def attend(pack, queries, chunks, marked, params, earlier):
    wide = queries.shape[2]
    row_spec = pl.BlockSpec((None, ROWS, wide), lambda i: (pack, 0, 0))
    in_specs, operands = [row_spec], [queries]
    for x in marked:
        for at in range(2 * ROWS, x.shape[0], MARKED_ROWS):
            in_specs.append(pl.BlockSpec((META, HD), lambda i, at=at // META: (at, 0)))
            operands.append(x)
    blocks = []
    for n, x in enumerate(chunks):
        blocks += [(n, at) for at in range(0, x.shape[0], 2 * ROWS if pack == 0 else MARKED_ROWS)]
        in_specs.append(pl.BlockSpec(x.shape, lambda i: (0, 0)))
        operands.append(x)
    in_specs.append(pl.BlockSpec((HD, PARAMS), lambda i: (0, 0)))
    operands.append(params)
    aliases = {}
    if earlier is not None:
        aliases = {len(operands): 0}
        operands.append(earlier)
        in_specs.append(pl.BlockSpec(memory_space=pl.ANY))
    span = WINDOW * ROWS
    return pl.pallas_call(
        functools.partial(attend_kernel, pack, tuple(blocks)),
        grid=(1,),
        in_specs=in_specs,
        out_specs=row_spec,
        out_shape=jax.ShapeDtypeStruct(queries.shape, queries.dtype),
        input_output_aliases=aliases,
        compiler_params=pltpu.CompilerParams(vmem_limit_bytes=40 * 1024 * 1024),
        cost_estimate=pl.CostEstimate(
            flops=KV * GROUP * ROWS * span * HD * 6,
            bytes_accessed=2 * ROWS * wide * 2 + span * KV * HD * 4,
            transcendentals=KV * GROUP * ROWS * span,
        ),
        name="attend",
    )(*operands)


def whole_block(shape):
    return pl.BlockSpec(shape, lambda i: (0,) * len(shape))


def collect_kernel(place_ref, keys_ref, values_ref, segments_ref, modality_ref, *outs):
    both_ref, a_ref, b_ref = outs
    wide = keys_ref.shape[2]
    row = lax.broadcasted_iota(jnp.int32, (META, wide), 0)
    marks = jnp.zeros((META, wide), jnp.int32)
    for p in range(2):
        documents = segments_ref[p : p + 1, :] + 1
        documents = jnp.concatenate([documents, jnp.zeros_like(documents)], axis=1)
        documents = jnp.concatenate([documents] * KV, axis=1)
        kind = jnp.broadcast_to(modality_ref[p : p + 1, 0:1], (1, wide))
        marks = jnp.where(row == MARKS * p, documents, marks)
        marks = jnp.where(row == MARKS * p + 1, kind, marks)
        marks = jnp.where(row == MARKS * p + 2, place_ref[0], marks)
    marks = marks.astype(jnp.float32).astype(both_ref.dtype)
    for p, ref in enumerate((a_ref, b_ref)):
        for at, source in ((0, keys_ref), (ROWS, values_ref)):
            rows = source[p]
            ref[at : at + ROWS, :] = rows
            both_ref[2 * ROWS * p + at : 2 * ROWS * p + at + ROWS, :] = rows
    b_ref[2 * ROWS :, :] = marks
    both_ref[4 * ROWS :, :] = marks


def collect(keys, values, segments, modality, place):
    wide = keys.shape[2]
    shapes = [(4 * ROWS + META, wide), (2 * ROWS, wide), (MARKED_ROWS, wide)]
    return pl.pallas_call(
        collect_kernel,
        grid=(1,),
        in_specs=[pl.BlockSpec(memory_space=pltpu.SMEM)]
        + [whole_block(x.shape) for x in (keys, values, segments, modality)],
        out_specs=[whole_block(shape) for shape in shapes],
        out_shape=[jax.ShapeDtypeStruct(shape, keys.dtype) for shape in shapes],
        compiler_params=pltpu.CompilerParams(vmem_limit_bytes=60 * 1024 * 1024),
        name="collect",
    )(place.astype(jnp.int32).reshape(1), keys, values, segments, modality)


def spread_kernel(*refs):
    out_ref = refs[-1]
    _, width, lanes = out_ref.shape
    parts = [ref[m] for ref in refs[:-1] for m in range(ref.shape[0])]
    filled = sum(part.shape[1] for part in parts)
    parts.append(jnp.zeros((width, lanes - filled), out_ref.dtype))
    out_ref[...] = jnp.broadcast_to(jnp.concatenate(parts, axis=1)[None], out_ref.shape)


def gather_params(*norms):
    copies = lax.axis_size("dp")
    norms = [x.transpose(0, 2, 1) for x in norms]
    width = norms[0].shape[1]
    shape = (copies, width, PARAMS)
    sent = pl.pallas_call(
        spread_kernel,
        grid=(1,),
        in_specs=[whole_block(x.shape) for x in norms],
        out_specs=whole_block(shape),
        out_shape=jax.ShapeDtypeStruct(shape, norms[0].dtype),
        compiler_params=pltpu.CompilerParams(vmem_limit_bytes=60 * 1024 * 1024),
        name="spread",
    )(*norms)
    whole = lax.all_to_all(sent, "dp", split_axis=0, concat_axis=0, tiled=True)
    return whole.reshape(copies * width, PARAMS)


def on_device(queries, keys, values, segments, modality, q_scale, q_shift, k_scale, k_shift):
    count = lax.axis_size("head")
    place = lax.axis_index("head")
    odd = place % 2 == 1
    swap = [(i, i ^ 1) for i in range(count)]
    ahead = pairs(range(count // 2 - 1), 1, count)

    def send(x, route):
        return lax.ppermute(x, "head", route)

    own, own_a, own_b = collect(keys, values, segments, modality, place)
    params = gather_params(q_scale, q_shift, k_scale, k_shift)
    first = send(own, ahead)
    sources = range(count // 2 - 4)
    back_b = send(own_b, pairs(sources, -2, count))
    first_a, first_b = first[: 2 * ROWS], first[2 * ROWS :]
    first_a, back_b = lax.optimization_barrier((first_a, back_b))
    second_a = send(first_a, ahead)
    second_b = send(first_b, ahead)
    fourth_b = send(back_b, pairs([z - 2 for z in sources], -2, count))
    second_a, params = lax.optimization_barrier((second_a, params))
    third_a = send(second_a, ahead)
    third_b = send(second_b, ahead)
    fourth_a = send(third_a, ahead)

    def crossed(own, first, second, third, fourth):
        lacking = jnp.where(odd, fourth, own)
        return send(jnp.concatenate([first, second, third, lacking], axis=0), swap)

    all_b = [own_b, first_b, second_b, third_b, fourth_b]
    all_b.append(crossed(*all_b))
    all_a = [own_a, first_a, second_a, third_a, fourth_a]
    all_a.append(crossed(*all_a))
    out = attend(1, queries, all_b, all_b, params, None)
    return attend(0, queries, all_a, all_b, params, out)


def solution(mesh):
    rows = P("dp", "head", None)
    marks = P("dp", "head")
    norms = P(None, None, "dp")
    placed = (rows, rows, rows, marks, marks, norms, norms, norms, norms)
    return jax.shard_map(
        on_device, mesh=mesh, in_specs=placed, out_specs=rows, check_vma=False
    )
```

```python
import functools
import math

import jax
import jax.numpy as jnp
from jax import lax
from jax.experimental import pallas as pl
from jax.experimental.pallas import tpu as pltpu
from jax.sharding import PartitionSpec as P

KV = 8
GROUP = 8
HD = 128
ROWS = 64
META = 16
MARKS = 3
MARKED_ROWS = 2 * ROWS + META
PARAMS = 384
WINDOW = 9
MASKED = -1e30


def pairs(chips, hops, count):
    ring = count // 2
    return [(2 * (z % ring) + c, 2 * ((z + hops) % ring) + c) for z in chips for c in (0, 1)]


def normed(x, gain, shift):
    center = x - jnp.mean(x, axis=-1, keepdims=True)
    spread = jnp.mean(center * center, axis=-1, keepdims=True)
    return (center * lax.rsqrt(spread + 1e-05) * gain + shift).astype(jnp.bfloat16)


def attend_kernel(pack, blocks, q_ref, *refs):
    meta_refs = refs[:WINDOW]
    chunks = [(refs[WINDOW + i], at) for i, at in blocks]
    params_ref = refs[WINDOW + 1 + blocks[-1][0]]
    out_ref = refs[-1]
    table = params_ref[...].T

    def pick(image, first, second):
        return jnp.where(image, table[second], table[first])

    marks = slice(MARKS * pack, MARKS * (pack + 1))
    metas = [ref[...].astype(jnp.float32)[marks] for ref in meta_refs]
    images = [meta[1:2] > 0.5 for meta in metas]

    span = ROWS * WINDOW
    key_seg = jnp.concatenate([meta[0:1, :ROWS] for meta in metas], axis=1)
    key_block = jnp.concatenate([meta[2:3, :ROWS] for meta in metas], axis=1)
    query_seg = jnp.broadcast_to(metas[0][0:1], (HD, HD)).T[:ROWS, 0:1]
    query_block = metas[0][2:3, 0:1]
    key_at = lax.broadcasted_iota(jnp.int32, (ROWS, span), 1)
    query_at = lax.broadcasted_iota(jnp.int32, (ROWS, span), 0)
    past = ((key_at >= ROWS) & (key_block < query_block)) | (key_at <= query_at)
    bias = jnp.where((query_seg == key_seg) & past, 0.0, MASKED)

    for j in range(KV):
        lanes = slice(j * HD, (j + 1) * HD)
        k_normed = []
        for (ref, at), image in zip(chunks, images):
            gain = pick(image, slice(256 + j, 257 + j), slice(264 + j, 265 + j))
            shift = pick(image, slice(272 + j, 273 + j), slice(280 + j, 281 + j))
            k_normed.append(normed(ref[at : at + ROWS, lanes].astype(jnp.float32), gain, shift))
        keys = jnp.concatenate(k_normed, axis=0)
        values = jnp.concatenate(
            [ref[at + ROWS : at + 2 * ROWS, lanes] for ref, at in chunks], axis=0
        )
        values = jnp.concatenate([values, jnp.ones_like(values)], axis=1)

        first = GROUP * j
        gains = pick(images[0], slice(first, first + 8), slice(64 + first, 72 + first))
        shifts = pick(images[0], slice(128 + first, 136 + first), slice(192 + first, 200 + first))
        queries = jnp.concatenate(
            [
                normed(
                    q_ref[:, (first + h) * HD : (first + h + 1) * HD].astype(jnp.float32),
                    gains[h : h + 1],
                    shifts[h : h + 1],
                )
                for h in range(GROUP)
            ],
            axis=0,
        )
        scores = lax.dot_general(
            queries, keys, (((1,), (1,)), ((), ())), preferred_element_type=jnp.float32
        ) * (HD**-0.5 * math.log2(math.e))
        scores = (scores.reshape(GROUP, ROWS, span) + bias[None]).reshape(GROUP * ROWS, span)
        weights = jnp.exp2(scores - jnp.max(scores, axis=-1, keepdims=True))
        mixed = jnp.dot(weights.astype(jnp.bfloat16), values, preferred_element_type=jnp.float32)
        result = (mixed[:, :HD] * (1.0 / mixed[:, HD:])).astype(out_ref.dtype)
        for h in range(GROUP):
            lane = (first + h) * HD
            out_ref[:, lane : lane + HD] = result[h * ROWS : (h + 1) * ROWS]


def attend(pack, queries, chunks, marked, params, earlier):
    wide = queries.shape[2]
    row_spec = pl.BlockSpec((None, ROWS, wide), lambda i: (pack, 0, 0))
    in_specs, operands = [row_spec], [queries]
    for x in marked:
        for at in range(2 * ROWS, x.shape[0], MARKED_ROWS):
            in_specs.append(pl.BlockSpec((META, HD), lambda i, at=at // META: (at, 0)))
            operands.append(x)
    blocks = []
    for n, x in enumerate(chunks):
        blocks += [(n, at) for at in range(0, x.shape[0], 2 * ROWS if pack == 0 else MARKED_ROWS)]
        in_specs.append(pl.BlockSpec(x.shape, lambda i: (0, 0)))
        operands.append(x)
    in_specs.append(pl.BlockSpec((HD, PARAMS), lambda i: (0, 0)))
    operands.append(params)
    aliases = {}
    if earlier is not None:
        aliases = {len(operands): 0}
        operands.append(earlier)
        in_specs.append(pl.BlockSpec(memory_space=pl.ANY))
    span = WINDOW * ROWS
    return pl.pallas_call(
        functools.partial(attend_kernel, pack, tuple(blocks)),
        grid=(1,),
        in_specs=in_specs,
        out_specs=row_spec,
        out_shape=jax.ShapeDtypeStruct(queries.shape, queries.dtype),
        input_output_aliases=aliases,
        compiler_params=pltpu.CompilerParams(vmem_limit_bytes=40 * 1024 * 1024),
        cost_estimate=pl.CostEstimate(
            flops=KV * GROUP * ROWS * span * HD * 6,
            bytes_accessed=2 * ROWS * wide * 2 + span * KV * HD * 4,
            transcendentals=KV * GROUP * ROWS * span,
        ),
        name="attend",
    )(*operands)


def whole_block(shape):
    return pl.BlockSpec(shape, lambda i: (0,) * len(shape))


def collect_kernel(place_ref, keys_ref, values_ref, segments_ref, modality_ref, *outs):
    both_ref, a_ref, b_ref = outs
    wide = keys_ref.shape[2]
    row = lax.broadcasted_iota(jnp.int32, (META, wide), 0)
    marks = jnp.zeros((META, wide), jnp.int32)
    for p in range(2):
        documents = segments_ref[p : p + 1, :] + 1
        documents = jnp.concatenate([documents, jnp.zeros_like(documents)], axis=1)
        documents = jnp.concatenate([documents] * KV, axis=1)
        kind = jnp.broadcast_to(modality_ref[p : p + 1, 0:1], (1, wide))
        marks = jnp.where(row == MARKS * p, documents, marks)
        marks = jnp.where(row == MARKS * p + 1, kind, marks)
        marks = jnp.where(row == MARKS * p + 2, place_ref[0], marks)
    marks = marks.astype(jnp.float32).astype(both_ref.dtype)
    for p, ref in enumerate((a_ref, b_ref)):
        for at, source in ((0, keys_ref), (ROWS, values_ref)):
            rows = source[p]
            ref[at : at + ROWS, :] = rows
            both_ref[2 * ROWS * p + at : 2 * ROWS * p + at + ROWS, :] = rows
    b_ref[2 * ROWS :, :] = marks
    both_ref[4 * ROWS :, :] = marks


def collect(keys, values, segments, modality, place):
    wide = keys.shape[2]
    shapes = [(4 * ROWS + META, wide), (2 * ROWS, wide), (MARKED_ROWS, wide)]
    return pl.pallas_call(
        collect_kernel,
        grid=(1,),
        in_specs=[pl.BlockSpec(memory_space=pltpu.SMEM)]
        + [whole_block(x.shape) for x in (keys, values, segments, modality)],
        out_specs=[whole_block(shape) for shape in shapes],
        out_shape=[jax.ShapeDtypeStruct(shape, keys.dtype) for shape in shapes],
        compiler_params=pltpu.CompilerParams(vmem_limit_bytes=60 * 1024 * 1024),
        name="collect",
    )(place.astype(jnp.int32).reshape(1), keys, values, segments, modality)


def spread_kernel(*refs):
    out_ref = refs[-1]
    _, width, lanes = out_ref.shape
    parts = [ref[m] for ref in refs[:-1] for m in range(ref.shape[0])]
    filled = sum(part.shape[1] for part in parts)
    parts.append(jnp.zeros((width, lanes - filled), out_ref.dtype))
    out_ref[...] = jnp.broadcast_to(jnp.concatenate(parts, axis=1)[None], out_ref.shape)


def gather_params(*norms):
    copies = lax.axis_size("dp")
    norms = [x.transpose(0, 2, 1) for x in norms]
    width = norms[0].shape[1]
    shape = (copies, width, PARAMS)
    sent = pl.pallas_call(
        spread_kernel,
        grid=(1,),
        in_specs=[whole_block(x.shape) for x in norms],
        out_specs=whole_block(shape),
        out_shape=jax.ShapeDtypeStruct(shape, norms[0].dtype),
        compiler_params=pltpu.CompilerParams(vmem_limit_bytes=60 * 1024 * 1024),
        name="spread",
    )(*norms)
    whole = lax.all_to_all(sent, "dp", split_axis=0, concat_axis=0, tiled=True)
    return whole.reshape(copies * width, PARAMS)


def on_device(queries, keys, values, segments, modality, q_scale, q_shift, k_scale, k_shift):
    count = lax.axis_size("head")
    place = lax.axis_index("head")
    odd = place % 2 == 1
    swap = [(i, i ^ 1) for i in range(count)]

    def ahead(hop):
        return pairs(range(hop - 1, count // 2 - 1), 1, count)

    def send(x, route):
        return lax.ppermute(x, "head", route)

    own, own_a, own_b = collect(keys, values, segments, modality, place)
    params = gather_params(q_scale, q_shift, k_scale, k_shift)
    first = send(own, ahead(1))
    sources = range(count // 2 - 4)
    back_b = send(own_b, pairs(sources, -2, count))
    first_a, first_b = first[: 2 * ROWS], first[2 * ROWS :]
    first_a, back_b = lax.optimization_barrier((first_a, back_b))
    second_a = send(first_a, ahead(2))
    second_b = send(first_b, ahead(2))
    fourth_b = send(back_b, pairs([z - 2 for z in sources], -2, count))
    second_a, params = lax.optimization_barrier((second_a, params))
    third_a = send(second_a, ahead(3))
    third_b = send(second_b, ahead(3))
    fourth_a = send(third_a, ahead(4))

    def crossed(own, first, second, third, fourth):
        lacking = jnp.where(odd, fourth, own)
        return send(jnp.concatenate([first, second, third, lacking], axis=0), swap)

    all_b = [own_b, first_b, second_b, third_b, fourth_b]
    all_b.append(crossed(*all_b))
    all_a = [own_a, first_a, second_a, third_a, fourth_a]
    all_a.append(crossed(*all_a))
    out = attend(1, queries, all_b, all_b, params, None)
    return attend(0, queries, all_a, all_b, params, out)


def solution(mesh):
    rows = P("dp", "head", None)
    marks = P("dp", "head")
    norms = P(None, None, "dp")
    placed = (rows, rows, rows, marks, marks, norms, norms, norms, norms)
    return jax.shard_map(
        on_device, mesh=mesh, in_specs=placed, out_specs=rows, check_vma=False
    )
```
